32 devices in a mesh: dp: 4 (over y, x), seq: 8 (over z, core).
Axes of the slice: x: 2, y: 2, z: 4, core: 2. Of those that a mesh axis runs over, the one named last changes fastest.
Arguments:
- hidden_in: bfloat16 [8, 1024, 896], P('dp', 'seq'), may hold values from -6 to 6
- segments: int32 [8, 1024], P('dp', 'seq'), may hold values from 0 to 3, as said below
- w_query: bfloat16 [802816], P(('dp', 'seq')), may hold values from -0.25 to 0.25
- w_key: bfloat16 [114688], P(('dp', 'seq')), may hold values from -0.25 to 0.25
- w_value: bfloat16 [114688], P(('dp', 'seq')), may hold values from -0.1875 to 0.1875
- w_out: bfloat16 [802816], P(('dp', 'seq')), may hold values from -0.75 to 0.75
- w_gate: bfloat16 [4358144], P(('dp', 'seq')), may hold values from -0.1875 to 0.1875
- w_up: bfloat16 [4358144], P(('dp', 'seq')), may hold values from -0.1875 to 0.1875
- w_down: bfloat16 [4358144], P(('dp', 'seq')), may hold values from -0.15625 to 0.15625
- gain_vector: bfloat16 [1792], P('seq'), may hold values from 0.099609375 to 1.8984375
- bias_vector: bfloat16 [1152], P('seq'), may hold values from -3 to 3
- out_grad: bfloat16 [8, 1024, 896], P('dp', 'seq'), may hold values from -6 to 6
Outputs:
- output: bfloat16 [8, 1024, 896], P('dp', 'seq')
- input_grad: float32 [8, 1024, 896], P('dp', 'seq')
- grad_query: float32 [802816], P(('dp', 'seq'))
- grad_key: float32 [114688], P(('dp', 'seq'))
- grad_value: float32 [114688], P(('dp', 'seq'))
- grad_out: float32 [802816], P(('dp', 'seq'))
- grad_gate: float32 [4358144], P(('dp', 'seq'))
- grad_up: float32 [4358144], P(('dp', 'seq'))
- grad_down: float32 [4358144], P(('dp', 'seq'))
- gain_grad: float32 [1792], P('seq')
- bias_grad: float32 [1152], P('seq')
The draws below stay inside these ranges and needn't reach their ends.
Inputs may be any that keep to these rules, and one draw needn't show every extreme that they name: `segments`: segment numbers start at 0 and never fall along a sequence. Of the 2 sequences of each dp index one, drawn from the seed, is a single document of 1024 tokens; every other sequence holds exactly 4 documents, each of 128 tokens or more.
All inputs are finite; a program needn't handle non-finite values.
Results may differ from the reference program's by a relative error of at most 0.015.
The reference program's roundings to bfloat16 on the way count: a program that leaves them out, or rounds other values in their place, can miss the bound.
Values may be sent and summed in bfloat16 or wider, within the bound.
A program may use at most 256 MiB of HBM per device.

```python
import math
import jax
import jax.numpy as jnp
from jax import lax

D = 896
HEADS = 14
KVH = 2
HD = 64
FF = 4864
KVW = 128
SEQS = 2
DOCS = 4
LENGTH = 1024
SEQ_ALL = 8


def draw_segments(key, part):
    key = jax.random.fold_in(key, 7)
    cut_key, pick_key = jax.random.split(key)
    shortest = LENGTH // (2 * DOCS)
    spare = LENGTH - DOCS * shortest
    offsets = jax.random.randint(cut_key, (SEQ_ALL, DOCS - 1), 0, spare + 1)
    offsets = jnp.sort(offsets, axis=-1).astype(jnp.int32)
    steps_in = (jnp.arange(DOCS - 1).astype(jnp.int32) + 1) * shortest
    cut_points = offsets + steps_in[None, :]
    places = jnp.arange(LENGTH).astype(jnp.int32)
    packed = jnp.sum((cut_points[:, None, :] <= places[None, :, None]).astype(jnp.int32), axis=-1)
    chosen = jax.random.randint(pick_key, (SEQ_ALL // SEQS,), 0, SEQS)
    row_index = jnp.arange(SEQ_ALL).astype(jnp.int32)
    single = row_index % SEQS == jnp.repeat(chosen, SEQS)
    return jnp.where(single[:, None], 0, packed).astype(jnp.int32)


def block_levels(key, shape, cuts, least, top_value):
    def one(position, blocks):
        steps = jax.random.uniform(jax.random.fold_in(jax.random.fold_in(key, 6), position), (blocks,), jnp.float32, least / len(cuts), top_value / len(cuts))
        return jnp.repeat(jnp.exp(steps), shape[position] // blocks).reshape((-1,) + (1,) * (len(shape) - position - 1))

    loudness = one(*cuts[0])
    for cut in cuts[1:]:
        loudness = loudness * one(*cut)
    return loudness


def gaussian(own_key, shape, width, reach, cuts=(), dtype=jnp.bfloat16):
    gain = block_levels(own_key, shape, cuts, -0.22, 0.18) if cuts else 1.0
    values = jax.random.normal(own_key, shape, jnp.float32) * width * gain
    return jnp.minimum(jnp.maximum(values, -reach), reach).astype(dtype)


def setup_inputs(seed: int = 0) -> dict:
    streams_of = jax.random.split(jax.random.key(seed), 13)
    hidden_in = gaussian(streams_of[0], (SEQ_ALL, LENGTH, D), 1.0, 6.0, ((0, 4), (1, 8)))
    segments = draw_segments(jax.random.fold_in(streams_of[12], 71), 0)
    w_query = gaussian(streams_of[2], (D * D,), (D // 2) ** -0.5, 0.25, ((0, 32),))
    w_key = gaussian(streams_of[3], (D * KVW,), (D // 2) ** -0.5, 0.25, ((0, 32),))
    w_value = gaussian(streams_of[4], (D * KVW,), D ** -0.5, 0.1875, ((0, 32),))
    w_out = gaussian(streams_of[5], (D * D,), (D // 16) ** -0.5, 0.75, ((0, 32),))
    w_gate = gaussian(streams_of[6], (D * FF,), D ** -0.5, 0.1875, ((0, 32),))
    w_up = gaussian(streams_of[7], (D * FF,), D ** -0.5, 0.1875, ((0, 32),))
    w_down = gaussian(streams_of[8], (FF * D,), (FF // 4) ** -0.5, 0.15625, ((0, 32),))
    gain_vector = jnp.clip(1.0 + 0.18 * jax.random.normal(streams_of[9], (2 * D,), jnp.float32), 0.099609375, 1.8984375).astype(jnp.bfloat16)
    bias_vector = gaussian(streams_of[10], (D + 2 * KVW,), 0.5, 3.0, ((0, 8),))
    out_grad = gaussian(streams_of[11], (SEQ_ALL, LENGTH, D), 1.0, 6.0, ((0, 4), (1, 8)))
    return dict(hidden_in=hidden_in, segments=segments, w_query=w_query, w_key=w_key, w_value=w_value, w_out=w_out, w_gate=w_gate, w_up=w_up, w_down=w_down, gain_vector=gain_vector, bias_vector=bias_vector, out_grad=out_grad)


EPSILON = 1e-06
ROPE_BASE = 1000000.0
MASKED = -1e+30
HIGH = lax.Precision.HIGHEST

@jax.custom_vjp
def low(v):
    return lax.optimization_barrier(v.astype(jnp.bfloat16)).astype(jnp.float32)

@jax.custom_vjp
def low_back(v):
    return v

def low_keep(v):
    return (low(v), None)

def low_pass(kept, grad):
    return (grad,)

def back_keep(v):
    return (v, None)

def back_low(kept, grad):
    return (low(grad),)
low.defvjp(low_keep, low_pass)
low_back.defvjp(back_keep, back_low)

def product(left, right):
    return jnp.dot(left, right, precision=HIGH)

def rms_norm(values, scaling):
    return values * lax.rsqrt(lax.optimization_barrier(jnp.mean(values * values, axis=-1, keepdims=True)) + EPSILON) * scaling

def rope_tables(places, head_size):
    half = head_size // 2
    freqs = jnp.exp(jnp.arange(half).astype(jnp.float32) * (-2.0 * math.log(ROPE_BASE) / head_size))
    angles = places.astype(jnp.float32)[..., None] * freqs
    cosine = jnp.cos(angles)
    sine = jnp.sin(angles)
    return (jnp.concatenate([cosine, cosine], axis=-1), jnp.concatenate([sine, sine], axis=-1))

def turn(values, cosine, sine):
    half = values.shape[-1] // 2
    turned = jnp.concatenate([-values[..., half:], values[..., :half]], axis=-1)
    return values * cosine + turned * sine

def doc_places(doc_ids):
    length = doc_ids.shape[-1]
    numbers = jnp.arange(DOCS).astype(jnp.int32)
    starts = lax.optimization_barrier(jnp.sum((doc_ids[..., :, None] < numbers).astype(jnp.int32), axis=-2))
    first_index = lax.optimization_barrier(jnp.sum(jnp.where(doc_ids[..., :, None] == numbers, starts[..., None, :], 0), axis=-1))
    return jnp.arange(length).astype(jnp.int32) - first_index

def layer_seq(inputs, doc_ids, query_mat, key_mat, value_mat, out_mat, gate_mat, up_mat, down_mat, gain_full, bias_full):
    length = inputs.shape[0]
    group_size = HEADS // KVH
    places = doc_places(doc_ids)
    cosine, sine = rope_tables(places, HD)
    indices = jnp.arange(length).astype(jnp.int32)
    allowed = (doc_ids[:, None] == doc_ids[None, :]) & (indices[None, :] <= indices[:, None])
    normed = low(rms_norm(inputs, gain_full[:D]))
    query = low_back(product(normed, query_mat) + bias_full[:D])
    key_low = low(low_back(product(normed, key_mat) + bias_full[D:D + KVW]))
    value_low = low(low_back(product(normed, value_mat) + bias_full[D + KVW:]))
    query = low(turn(query.reshape(length, HEADS, HD).transpose(1, 0, 2), cosine, sine))
    key_rot = low(turn(key_low.reshape(length, KVH, HD).transpose(1, 0, 2), cosine, sine))
    value_heads = value_low.reshape(length, KVH, HD).transpose(1, 0, 2)
    grouped = query.reshape(KVH, group_size, length, HD)

    def attend(pieces):
        query_block, key_block, value_block = pieces
        scores = low_back(jnp.einsum('gqd,kd->gqk', query_block, key_block, precision=HIGH) * HD ** (-0.5))
        scores = jnp.where(allowed, scores, MASKED)
        highest = lax.optimization_barrier(jnp.max(scores, axis=-1, keepdims=True))
        weights = jnp.exp(scores - highest)
        shares = low(weights / lax.optimization_barrier(jnp.sum(weights, axis=-1, keepdims=True)))
        return jnp.einsum('gqk,kd->gqd', shares, value_block, precision=HIGH)
    mixed_heads = lax.map(jax.checkpoint(attend), (grouped, key_rot, value_heads))
    mixed_rows = mixed_heads.reshape(HEADS, length, HD).transpose(1, 0, 2).reshape(length, D)
    mixed_rows = low(low_back(mixed_rows))
    middle = inputs + low_back(product(mixed_rows, out_mat))
    normed_two = low(rms_norm(middle, gain_full[D:]))
    gate_pre = low_back(product(normed_two, gate_mat))
    up_pre = low_back(product(normed_two, up_mat))
    activated = low(jax.nn.silu(gate_pre) * up_pre)
    return middle + low_back(product(activated, down_mat))

def reference(hidden_in, segments, w_query, w_key, w_value, w_out, w_gate, w_up, w_down, gain_vector, bias_vector, out_grad):
    params = (w_query.astype(jnp.float32).reshape(D, D), w_key.astype(jnp.float32).reshape(D, KVW), w_value.astype(jnp.float32).reshape(D, KVW), w_out.astype(jnp.float32).reshape(D, D), w_gate.astype(jnp.float32).reshape(D, FF), w_up.astype(jnp.float32).reshape(D, FF), w_down.astype(jnp.float32).reshape(FF, D), gain_vector.astype(jnp.float32), bias_vector.astype(jnp.float32))

    def whole(inputs, *weights):

        def one_seq(pair):
            return jax.checkpoint(layer_seq)(pair[0], pair[1], *weights)
        return lax.map(one_seq, (inputs, segments))
    result, pull = jax.vjp(whole, hidden_in.astype(jnp.float32), *params)
    grads = pull(out_grad.astype(jnp.float32))
    return (result.astype(jnp.bfloat16), grads[0], grads[1].reshape(-1), grads[2].reshape(-1), grads[3].reshape(-1), grads[4].reshape(-1), grads[5].reshape(-1), grads[6].reshape(-1), grads[7].reshape(-1), grads[8], grads[9])
```

```python
import math

import jax
import jax.numpy as jnp
from jax import lax
from jax.sharding import PartitionSpec as P

D = 896
HEADS = 14
KVH = 2
HD = 64
FF = 4864
KVW = 128
DOCS = 4


EPSILON = 1e-06
ROPE_BASE = 1000000.0
MASKED = -1e30


def rms_norm(values, scaling):
    return values * lax.rsqrt(jnp.mean(values * values, axis=-1, keepdims=True) + EPSILON) * scaling


def rope_tables(places, head_size):
    half = head_size // 2
    freqs = jnp.exp(jnp.arange(half).astype(jnp.float32) * (-2.0 * math.log(ROPE_BASE) / head_size))
    angles = places.astype(jnp.float32)[..., None] * freqs
    cosine = jnp.cos(angles)
    sine = jnp.sin(angles)
    return (jnp.concatenate([cosine, cosine], axis=-1), jnp.concatenate([sine, sine], axis=-1))


def turn(values, cosine, sine):
    half = values.shape[-1] // 2
    turned = jnp.concatenate([-values[..., half:], values[..., :half]], axis=-1)
    return values * cosine + turned * sine


def unturn(gradient, cosine, sine):
    half = gradient.shape[-1] // 2
    scaled = gradient * sine
    return gradient * cosine + jnp.concatenate([scaled[..., half:], -scaled[..., :half]], axis=-1)


def doc_places(doc_ids):
    length = doc_ids.shape[-1]
    numbers = jnp.arange(DOCS)
    starts = jnp.sum((doc_ids[..., :, None] < numbers).astype(jnp.int32), axis=-2)
    first_index = jnp.sum(
        jnp.where(doc_ids[..., :, None] == numbers, starts[..., None, :], 0), axis=-1
    )
    return jnp.arange(length) - first_index


def gated(gate_part, up_part):
    return jax.nn.silu(gate_part) * up_part


def matmul(left, right):
    return jnp.dot(left, right, preferred_element_type=jnp.float32)


def contract_last(left, right):
    return lax.dot_general(
        left, right, (((1,), (1,)), ((), ())), preferred_element_type=jnp.float32
    )


def contract_first(left, right):
    return lax.dot_general(
        left, right, (((0,), (0,)), ((), ())), preferred_element_type=jnp.float32
    )


def unflatten(pieces):
    return (
        pieces[0].reshape(D, D),
        pieces[1].reshape(D, KVW),
        pieces[2].reshape(D, KVW),
        pieces[3].reshape(D, D),
        pieces[4].reshape(D, FF),
        pieces[5].reshape(D, FF),
        pieces[6].reshape(FF, D),
    )


def masked_scores(queries, key_rows, allowed):
    scores = jnp.einsum(
        "hgqd,hld->hgql", queries, key_rows, preferred_element_type=jnp.float32
    ) * HD ** (-0.5)
    return jnp.where(allowed, scores, MASKED)


def attend_forward(pieces):
    queries, key_rows, values, allowed = pieces
    scores = masked_scores(queries, key_rows, allowed)
    highest = jnp.max(scores, axis=-1, keepdims=True)
    weights = jnp.exp(scores - highest)
    summed = jnp.sum(weights, axis=-1, keepdims=True)
    shares = (weights / summed).astype(jnp.bfloat16)
    mixed_heads = jnp.einsum("hgql,hld->hgqd", shares, values, preferred_element_type=jnp.float32)
    return (mixed_heads, (highest + jnp.log(summed))[..., 0])


def attend_backward(pieces):
    queries, key_rows, values, allowed, log_total, grad_mixed = pieces
    scores = masked_scores(queries, key_rows, allowed)
    shares = jnp.exp(scores - log_total[..., None])
    shares_low = shares.astype(jnp.bfloat16)
    grad_shares = jnp.einsum(
        "hgqd,hld->hgql", grad_mixed, values, preferred_element_type=jnp.float32
    )
    inner = jnp.sum(shares * grad_shares, axis=-1, keepdims=True)
    grad_scores = (shares * (grad_shares - inner)).astype(jnp.bfloat16)
    score_scale = HD ** (-0.5)
    grad_queries = (
        jnp.einsum("hgql,hld->hgqd", grad_scores, key_rows, preferred_element_type=jnp.float32)
        * score_scale
    )
    grad_keys = (
        jnp.einsum("hgql,hgqd->hld", grad_scores, queries, preferred_element_type=jnp.float32)
        * score_scale
    )
    grad_values = jnp.einsum(
        "hgql,hgqd->hld", shares_low, grad_mixed, preferred_element_type=jnp.float32
    )
    return (grad_queries, grad_keys, grad_values)


def shards_flat(
    hidden_in,
    segments,
    w_query,
    w_key,
    w_value,
    w_out,
    w_gate,
    w_up,
    w_down,
    gain_vector,
    bias_vector,
    out_grad,
):
    seq_count = hidden_in.shape[0]
    block_len = hidden_in.shape[1]
    seq_len = block_len * lax.axis_size("seq")
    offset = lax.axis_index("seq") * block_len
    row_count = seq_count * block_len
    group_size = HEADS // KVH
    weights = unflatten(
        (
            lax.all_gather(w_query, ("dp", "seq"), axis=0, tiled=True),
            lax.all_gather(w_key, ("dp", "seq"), axis=0, tiled=True),
            lax.all_gather(w_value, ("dp", "seq"), axis=0, tiled=True),
            lax.all_gather(w_out, ("dp", "seq"), axis=0, tiled=True),
            lax.all_gather(w_gate, ("dp", "seq"), axis=0, tiled=True),
            lax.all_gather(w_up, ("dp", "seq"), axis=0, tiled=True),
            lax.all_gather(w_down, ("dp", "seq"), axis=0, tiled=True),
        )
    )
    query_mat, key_mat, value_mat, out_mat, gate_mat, up_mat, down_mat = weights
    gain_full, bias_full = (
        lax.all_gather(gain_vector, "seq", axis=0, tiled=True),
        lax.all_gather(bias_vector, "seq", axis=0, tiled=True),
    )
    first_gain = gain_full[:D].astype(jnp.float32)
    second_gain = gain_full[D:].astype(jnp.float32)
    bias_wide = bias_full.astype(jnp.float32)
    doc_all = lax.all_gather(segments, "seq", axis=1, tiled=True)
    places_all = doc_places(doc_all)
    cos_all, sin_all = rope_tables(places_all, HD)
    cos_here = lax.dynamic_slice_in_dim(cos_all, offset, block_len, 1)
    sin_here = lax.dynamic_slice_in_dim(sin_all, offset, block_len, 1)
    key_index = jnp.arange(seq_len)
    query_index = offset + jnp.arange(block_len)
    allowed = (segments[:, :, None] == doc_all[:, None, :]) & (
        key_index[None, None, :] <= query_index[None, :, None]
    )
    inputs = hidden_in.astype(jnp.float32).reshape(row_count, D)
    normed = rms_norm(inputs, first_gain).astype(jnp.bfloat16)
    query_pre = matmul(normed, query_mat) + bias_wide[:D]
    key_low = (
        (matmul(normed, key_mat) + bias_wide[D : D + KVW])
        .astype(jnp.bfloat16)
        .reshape(seq_count, block_len, KVW)
    )
    value_low = (
        (matmul(normed, value_mat) + bias_wide[D + KVW :])
        .astype(jnp.bfloat16)
        .reshape(seq_count, block_len, KVW)
    )
    key_all, value_all = (
        lax.all_gather(key_low, "seq", axis=1, tiled=True),
        lax.all_gather(value_low, "seq", axis=1, tiled=True),
    )
    key_heads = (
        key_all.astype(jnp.float32).reshape(seq_count, seq_len, KVH, HD).transpose(0, 2, 1, 3)
    )
    key_rot = turn(key_heads, cos_all[:, None], sin_all[:, None]).astype(jnp.bfloat16)
    value_heads = value_all.reshape(seq_count, seq_len, KVH, HD).transpose(0, 2, 1, 3)
    query_heads = query_pre.reshape(seq_count, block_len, KVH, group_size, HD).transpose(
        0, 2, 3, 1, 4
    )
    query_rot = turn(query_heads, cos_here[:, None, None], sin_here[:, None, None]).astype(
        jnp.bfloat16
    )
    mixed_heads, log_total = lax.map(attend_forward, (query_rot, key_rot, value_heads, allowed))
    mixed_rows = mixed_heads.transpose(0, 3, 1, 2, 4).reshape(row_count, D).astype(jnp.bfloat16)
    middle = inputs + matmul(mixed_rows, out_mat)
    normed_two = rms_norm(middle, second_gain).astype(jnp.bfloat16)
    gate_pre = matmul(normed_two, gate_mat)
    up_pre = matmul(normed_two, up_mat)
    activated = gated(gate_pre, up_pre).astype(jnp.bfloat16)
    result = middle + matmul(activated, down_mat)
    output = result.astype(jnp.bfloat16).reshape(seq_count, block_len, D)
    back_weights = unflatten(
        (
            lax.all_gather(w_query, ("dp", "seq"), axis=0, tiled=True),
            lax.all_gather(w_key, ("dp", "seq"), axis=0, tiled=True),
            lax.all_gather(w_value, ("dp", "seq"), axis=0, tiled=True),
            lax.all_gather(w_out, ("dp", "seq"), axis=0, tiled=True),
            lax.all_gather(w_gate, ("dp", "seq"), axis=0, tiled=True),
            lax.all_gather(w_up, ("dp", "seq"), axis=0, tiled=True),
            lax.all_gather(w_down, ("dp", "seq"), axis=0, tiled=True),
        )
    )
    query_mat, key_mat, value_mat, out_mat, gate_mat, up_mat, down_mat = back_weights
    grad_result = out_grad.astype(jnp.float32).reshape(row_count, D)
    grad_branch = grad_result.astype(jnp.bfloat16)
    grad_down_mat = contract_first(activated, grad_branch)
    grad_act = contract_last(grad_branch, down_mat)
    grad_gate_pre, grad_up_pre = jax.vjp(gated, gate_pre, up_pre)[1](grad_act)
    grad_gate_low = grad_gate_pre.astype(jnp.bfloat16)
    grad_up_low = grad_up_pre.astype(jnp.bfloat16)
    grad_gate_mat = contract_first(normed_two, grad_gate_low)
    grad_up_mat = contract_first(normed_two, grad_up_low)
    grad_normed_two = contract_last(grad_gate_low, gate_mat) + contract_last(grad_up_low, up_mat)
    grad_middle_part, grad_second_gain = jax.vjp(rms_norm, middle, second_gain)[1](grad_normed_two)
    grad_middle = grad_result + grad_middle_part
    grad_attn = grad_middle.astype(jnp.bfloat16)
    grad_out_mat = contract_first(mixed_rows, grad_attn)
    grad_mixed = contract_last(grad_attn, out_mat).astype(jnp.bfloat16)
    grad_mixed = grad_mixed.reshape(seq_count, block_len, KVH, group_size, HD).transpose(
        0, 2, 3, 1, 4
    )
    grad_query_rot, grad_key_rot, grad_value_heads = lax.map(
        attend_backward, (query_rot, key_rot, value_heads, allowed, log_total, grad_mixed)
    )
    grad_query_pre = unturn(grad_query_rot, cos_here[:, None, None], sin_here[:, None, None])
    grad_query_low = (
        grad_query_pre.transpose(0, 3, 1, 2, 4).reshape(row_count, D).astype(jnp.bfloat16)
    )
    grad_key_all = (
        unturn(grad_key_rot, cos_all[:, None], sin_all[:, None])
        .transpose(0, 2, 1, 3)
        .reshape(seq_count, seq_len, KVW)
    )
    grad_value_all = grad_value_heads.transpose(0, 2, 1, 3).reshape(seq_count, seq_len, KVW)
    grad_key_sum, grad_value_sum = (
        lax.psum_scatter(
            grad_key_all.astype(jnp.bfloat16), "seq", scatter_dimension=1, tiled=True
        ).astype(jnp.float32),
        lax.psum_scatter(
            grad_value_all.astype(jnp.bfloat16), "seq", scatter_dimension=1, tiled=True
        ).astype(jnp.float32),
    )
    grad_key_low = grad_key_sum.reshape(row_count, KVW).astype(jnp.bfloat16)
    grad_value_low = grad_value_sum.reshape(row_count, KVW).astype(jnp.bfloat16)
    grad_query_mat = contract_first(normed, grad_query_low)
    grad_key_mat = contract_first(normed, grad_key_low)
    grad_value_mat = contract_first(normed, grad_value_low)
    grad_normed = (
        contract_last(grad_query_low, query_mat)
        + contract_last(grad_key_low, key_mat)
        + contract_last(grad_value_low, value_mat)
    )
    grad_inputs_part, grad_first_gain = jax.vjp(rms_norm, inputs, first_gain)[1](grad_normed)
    input_grad = (grad_middle + grad_inputs_part).reshape(seq_count, block_len, D)
    count_dp = lax.axis_size("dp")
    count_seq = lax.axis_size("seq")
    owners = count_dp * count_seq
    owned = (
        lax.psum_scatter(
            grad_query_mat.reshape(owners, -1), ("dp", "seq"), scatter_dimension=0, tiled=True
        ),
        lax.psum_scatter(
            grad_key_mat.reshape(owners, -1), ("dp", "seq"), scatter_dimension=0, tiled=True
        ),
        lax.psum_scatter(
            grad_value_mat.reshape(owners, -1), ("dp", "seq"), scatter_dimension=0, tiled=True
        ),
        lax.psum_scatter(
            grad_out_mat.reshape(owners, -1), ("dp", "seq"), scatter_dimension=0, tiled=True
        ),
        lax.psum_scatter(
            grad_gate_mat.reshape(owners, -1), ("dp", "seq"), scatter_dimension=0, tiled=True
        ),
        lax.psum_scatter(
            grad_up_mat.reshape(owners, -1), ("dp", "seq"), scatter_dimension=0, tiled=True
        ),
        lax.psum_scatter(
            grad_down_mat.reshape(owners, -1), ("dp", "seq"), scatter_dimension=0, tiled=True
        ),
    )
    summed = tuple((piece.reshape(-1) for piece in owned))
    gain_total = jnp.concatenate([grad_first_gain, grad_second_gain])
    bias_total = jnp.concatenate(
        [
            jnp.sum(grad_query_low.astype(jnp.float32), axis=0),
            jnp.sum(grad_key_low.astype(jnp.float32), axis=0),
            jnp.sum(grad_value_low.astype(jnp.float32), axis=0),
        ]
    )
    gain_sum, bias_sum = lax.psum((gain_total, bias_total), ("dp", "seq"))
    seq_index = lax.axis_index("seq")
    gain_piece = gain_vector.shape[0]
    bias_piece = bias_vector.shape[0]
    gain_grad = lax.dynamic_slice_in_dim(gain_sum, seq_index * gain_piece, gain_piece)
    bias_grad = lax.dynamic_slice_in_dim(bias_sum, seq_index * bias_piece, bias_piece)
    return (
        output,
        input_grad,
        summed[0],
        summed[1],
        summed[2],
        summed[3],
        summed[4],
        summed[5],
        summed[6],
        gain_grad,
        bias_grad,
    )


def spread(rows, block, spare):
    place = jnp.arange(rows)
    place = place // block * spare + place % block
    width = rows // block * spare
    return (place[:, None] == jnp.arange(width)[None, :]).astype(jnp.bfloat16)


def round_up(value, step):
    return -(-value // step) * step


def shards_split(
    hidden_in,
    segments,
    w_query,
    w_key,
    w_value,
    w_out,
    w_gate,
    w_up,
    w_down,
    gain_vector,
    bias_vector,
    out_grad,
):
    low = jnp.bfloat16
    seq_count, block_len, _ = hidden_in.shape
    count_dp = lax.axis_size("dp")
    count_seq = lax.axis_size("seq")
    owners = count_dp * count_seq
    dp_index = lax.axis_index("dp")
    seq_index = lax.axis_index("seq")
    seq_len = block_len * count_seq
    offset = seq_index * block_len
    row_count = seq_count * block_len
    group_size = HEADS // KVH
    own_rows = D // owners
    block = round_up(own_rows + 1, 16)
    own_units = FF // owners
    unit_block = round_up(own_units, 16)
    units = count_dp * unit_block
    gain_piece = gain_vector.shape[0]
    bias_piece = bias_vector.shape[0]
    both = ("dp", "seq")

    attn_width = 2 * D + 2 * KVW
    attn_rows = jnp.concatenate(
        [
            w_query.reshape(own_rows, D),
            w_key.reshape(own_rows, KVW),
            w_value.reshape(own_rows, KVW),
            w_out.reshape(own_rows, D),
        ],
        axis=1,
    )
    small = jnp.concatenate([gain_vector, bias_vector, segments.astype(low).reshape(-1)])
    small = jnp.pad(small, (0, attn_width - small.shape[0]))[None]
    attn_rows = jnp.concatenate(
        [attn_rows, small, jnp.zeros((block - own_rows - 1, attn_width), low)], axis=0
    )
    attn_all = lax.all_gather(attn_rows, both, axis=0, tiled=True)
    small_all = attn_all.reshape(owners, block, attn_width)[:, own_rows]
    gain_full = small_all[:count_seq, :gain_piece].reshape(-1).astype(jnp.float32)
    bias_wide = (
        small_all[:count_seq, gain_piece : gain_piece + bias_piece].reshape(-1).astype(jnp.float32)
    )
    small_here = lax.dynamic_slice_in_dim(small_all, dp_index * count_seq, count_seq, 0)
    doc_all = (
        small_here[:, gain_piece + bias_piece : gain_piece + bias_piece + row_count]
        .astype(jnp.int32)
        .reshape(count_seq, seq_count, block_len)
        .transpose(1, 0, 2)
        .reshape(seq_count, seq_len)
    )
    first_gain = gain_full[:D]
    second_gain = gain_full[D:]
    pick = spread(D, own_rows, block)
    attn_mat = matmul(pick, attn_all).astype(low)
    qkv_mat = attn_mat[:, : D + 2 * KVW]
    out_mat = attn_mat[:, D + 2 * KVW :]

    def by_user(flat):
        parts = flat.reshape(own_rows, count_dp, count_seq, own_units).transpose(2, 0, 1, 3)
        parts = jnp.pad(
            parts, ((0, 0), (0, block - own_rows), (0, 0), (0, unit_block - own_units))
        )
        return parts.reshape(count_seq, block, units)

    gate_up_own = jnp.concatenate([by_user(w_gate), by_user(w_up)], axis=2)
    gate_up_own = lax.all_to_all(gate_up_own, "seq", 0, 0, tiled=True)
    gate_up_all = lax.all_gather(
        gate_up_own.reshape(count_seq * block, 2 * units), "dp", axis=0, tiled=True
    )
    gate_up_mat = matmul(pick, gate_up_all).astype(low)
    down_own = jnp.pad(w_down.reshape(own_units, D), ((0, unit_block - own_units), (0, 0)))
    down_mat = lax.all_gather(down_own, "dp", axis=0, tiled=True)
    grad_branch_all = lax.all_gather(out_grad.reshape(row_count, D), "seq", axis=0, tiled=True)

    places_all = doc_places(doc_all)
    cos_all, sin_all = rope_tables(places_all, HD)
    cos_here = lax.dynamic_slice_in_dim(cos_all, offset, block_len, 1)
    sin_here = lax.dynamic_slice_in_dim(sin_all, offset, block_len, 1)
    key_index = jnp.arange(seq_len)
    query_index = offset + jnp.arange(block_len)
    allowed = (segments[:, :, None] == doc_all[:, None, :]) & (
        key_index[None, None, :] <= query_index[None, :, None]
    )
    inputs = hidden_in.astype(jnp.float32).reshape(row_count, D)
    normed = rms_norm(inputs, first_gain).astype(low)
    qkv_pre = matmul(normed, qkv_mat) + bias_wide
    query_pre = qkv_pre[:, :D]
    key_value_low = qkv_pre[:, D:].astype(low).reshape(seq_count, block_len, 2 * KVW)
    key_value_all = lax.all_gather(key_value_low, "seq", axis=1, tiled=True)
    key_all = key_value_all[..., :KVW]
    value_all = key_value_all[..., KVW:]
    key_heads = (
        key_all.astype(jnp.float32).reshape(seq_count, seq_len, KVH, HD).transpose(0, 2, 1, 3)
    )
    key_rot = turn(key_heads, cos_all[:, None], sin_all[:, None]).astype(low)
    value_heads = value_all.reshape(seq_count, seq_len, KVH, HD).transpose(0, 2, 1, 3)
    query_heads = query_pre.reshape(seq_count, block_len, KVH, group_size, HD).transpose(
        0, 2, 3, 1, 4
    )
    query_rot = turn(query_heads, cos_here[:, None, None], sin_here[:, None, None]).astype(low)
    mixed_heads, log_total = lax.map(attend_forward, (query_rot, key_rot, value_heads, allowed))
    mixed_rows = mixed_heads.transpose(0, 3, 1, 2, 4).reshape(row_count, D).astype(low)
    middle = inputs + matmul(mixed_rows, out_mat)
    normed_two = rms_norm(middle, second_gain).astype(low)

    normed_all = lax.all_gather(normed_two, "seq", axis=0, tiled=True)
    gate_up_pre = matmul(normed_all, gate_up_mat)
    gate_pre = gate_up_pre[:, :units]
    up_pre = gate_up_pre[:, units:]
    activated = gated(gate_pre, up_pre).astype(low)
    grad_act = contract_last(grad_branch_all, down_mat)
    grad_gate_pre, grad_up_pre = jax.vjp(gated, gate_pre, up_pre)[1](grad_act)
    grad_gate_up = jnp.concatenate([grad_gate_pre.astype(low), grad_up_pre.astype(low)], axis=1)
    grad_normed_part = contract_last(grad_gate_up, gate_up_mat).astype(low)
    grad_normed_two = lax.psum_scatter(
        grad_normed_part, "seq", scatter_dimension=0, tiled=True
    ).astype(jnp.float32)
    branch_part = matmul(activated, down_mat).astype(low)
    branch = lax.psum_scatter(branch_part, "seq", scatter_dimension=0, tiled=True)
    output = (middle + branch.astype(jnp.float32)).astype(low).reshape(seq_count, block_len, D)

    grad_gate_up_mat = contract_first(normed_all, grad_gate_up).astype(low)
    grad_gate_up_mat = contract_first(pick, grad_gate_up_mat).astype(low)
    grad_down_mat = contract_first(activated, grad_branch_all).astype(low)
    grad_gate_up_sum = lax.psum_scatter(grad_gate_up_mat, "dp", scatter_dimension=0, tiled=True)
    grad_down_sum = lax.psum_scatter(grad_down_mat, "dp", scatter_dimension=0, tiled=True)
    grad_down = grad_down_sum[:own_units].astype(jnp.float32).reshape(-1)
    grad_gate_up_own = lax.all_to_all(
        grad_gate_up_sum.reshape(count_seq, block, 2 * units), "seq", 0, 0, tiled=True
    )
    grad_gate_up_own = (
        grad_gate_up_own[:, :own_rows]
        .reshape(count_seq, own_rows, 2, count_dp, unit_block)[..., :own_units]
        .transpose(2, 1, 3, 0, 4)
        .reshape(2, -1)
        .astype(jnp.float32)
    )

    grad_result = out_grad.astype(jnp.float32).reshape(row_count, D)
    grad_middle_part, grad_second_gain = jax.vjp(rms_norm, middle, second_gain)[1](grad_normed_two)
    grad_middle = grad_result + grad_middle_part
    grad_attn = grad_middle.astype(low)
    pick_rows = lambda values: matmul(values, pick).astype(low)
    grad_out_mat = contract_first(pick_rows(mixed_rows), grad_attn).astype(low)
    grad_out_sum = lax.psum_scatter(grad_out_mat, both, scatter_dimension=0, tiled=True)
    grad_mixed = contract_last(grad_attn, out_mat).astype(low)
    grad_mixed = grad_mixed.reshape(seq_count, block_len, KVH, group_size, HD).transpose(
        0, 2, 3, 1, 4
    )
    grad_query_rot, grad_key_rot, grad_value_heads = lax.map(
        attend_backward, (query_rot, key_rot, value_heads, allowed, log_total, grad_mixed)
    )
    grad_query_pre = unturn(grad_query_rot, cos_here[:, None, None], sin_here[:, None, None])
    grad_query_low = grad_query_pre.transpose(0, 3, 1, 2, 4).reshape(row_count, D).astype(low)
    grad_key_all = (
        unturn(grad_key_rot, cos_all[:, None], sin_all[:, None])
        .transpose(0, 2, 1, 3)
        .reshape(seq_count, seq_len, KVW)
    )
    grad_value_all = grad_value_heads.transpose(0, 2, 1, 3).reshape(seq_count, seq_len, KVW)
    grad_key_value = jnp.concatenate([grad_key_all, grad_value_all], axis=-1).astype(low)
    grad_key_value_low = lax.psum_scatter(
        grad_key_value, "seq", scatter_dimension=1, tiled=True
    ).reshape(row_count, 2 * KVW)
    grad_qkv_low = jnp.concatenate([grad_query_low, grad_key_value_low], axis=1)
    grad_qkv_mat = contract_first(pick_rows(normed), grad_qkv_low)
    grad_normed = contract_last(grad_qkv_low, qkv_mat)
    grad_inputs_part, grad_first_gain = jax.vjp(rms_norm, inputs, first_gain)[1](grad_normed)
    input_grad = (grad_middle + grad_inputs_part).reshape(seq_count, block_len, D)
    gain_total = jnp.concatenate([grad_first_gain, grad_second_gain]).reshape(count_seq, gain_piece)
    bias_total = jnp.sum(grad_qkv_low.astype(jnp.float32), axis=0).reshape(count_seq, bias_piece)
    gain_sum, bias_sum = lax.psum((gain_total, bias_total), both)
    gain_grad = lax.dynamic_slice_in_dim(gain_sum, seq_index, 1, 0).reshape(-1)
    bias_grad = lax.dynamic_slice_in_dim(bias_sum, seq_index, 1, 0).reshape(-1)
    grad_qkv_sum = lax.psum_scatter(
        grad_qkv_mat.astype(low), both, scatter_dimension=0, tiled=True
    )[:own_rows].astype(jnp.float32)
    return (
        output,
        input_grad,
        grad_qkv_sum[:, :D].reshape(-1),
        grad_qkv_sum[:, D : D + KVW].reshape(-1),
        grad_qkv_sum[:, D + KVW :].reshape(-1),
        grad_out_sum[:own_rows].astype(jnp.float32).reshape(-1),
        grad_gate_up_own[0],
        grad_gate_up_own[1],
        grad_down,
        gain_grad,
        bias_grad,
    )


def solution(mesh):
    in_specs = (
        P("dp", "seq", None),
        P("dp", "seq"),
        P(("dp", "seq")),
        P(("dp", "seq")),
        P(("dp", "seq")),
        P(("dp", "seq")),
        P(("dp", "seq")),
        P(("dp", "seq")),
        P(("dp", "seq")),
        P("seq"),
        P("seq"),
        P("dp", "seq", None),
    )
    out_specs = (
        P("dp", "seq", None),
        P("dp", "seq", None),
        P(("dp", "seq")),
        P(("dp", "seq")),
        P(("dp", "seq")),
        P(("dp", "seq")),
        P(("dp", "seq")),
        P(("dp", "seq")),
        P(("dp", "seq")),
        P("seq"),
        P("seq"),
    )
    owners = mesh.size
    whole_rows = D % owners == 0 and FF % owners == 0
    shards = shards_split if whole_rows else shards_flat
    return jax.shard_map(shards, mesh=mesh, in_specs=in_specs, out_specs=out_specs, check_vma=False)
```

```python
import math

import jax
import jax.numpy as jnp
from jax import lax
from jax.sharding import PartitionSpec as P

D = 896
HEADS = 14
KVH = 2
HD = 64
FF = 4864
KVW = 128
DOCS = 4


EPSILON = 1e-06
ROPE_BASE = 1000000.0
MASKED = -1e30


def rms_norm(values, scaling):
    return values * lax.rsqrt(jnp.mean(values * values, axis=-1, keepdims=True) + EPSILON) * scaling


def rope_tables(places, head_size):
    half = head_size // 2
    freqs = jnp.exp(jnp.arange(half).astype(jnp.float32) * (-2.0 * math.log(ROPE_BASE) / head_size))
    angles = places.astype(jnp.float32)[..., None] * freqs
    cosine = jnp.cos(angles)
    sine = jnp.sin(angles)
    return (jnp.concatenate([cosine, cosine], axis=-1), jnp.concatenate([sine, sine], axis=-1))


def turn(values, cosine, sine):
    half = values.shape[-1] // 2
    turned = jnp.concatenate([-values[..., half:], values[..., :half]], axis=-1)
    return values * cosine + turned * sine


def unturn(gradient, cosine, sine):
    half = gradient.shape[-1] // 2
    scaled = gradient * sine
    return gradient * cosine + jnp.concatenate([scaled[..., half:], -scaled[..., :half]], axis=-1)


def doc_places(doc_ids):
    length = doc_ids.shape[-1]
    numbers = jnp.arange(DOCS)
    starts = jnp.sum((doc_ids[..., :, None] < numbers).astype(jnp.int32), axis=-2)
    first_index = jnp.sum(
        jnp.where(doc_ids[..., :, None] == numbers, starts[..., None, :], 0), axis=-1
    )
    return jnp.arange(length) - first_index


def gated(gate_part, up_part):
    return jax.nn.silu(gate_part) * up_part


def matmul(left, right):
    return jnp.dot(left, right, preferred_element_type=jnp.float32)


def contract_last(left, right):
    return lax.dot_general(
        left, right, (((1,), (1,)), ((), ())), preferred_element_type=jnp.float32
    )


def contract_first(left, right):
    return lax.dot_general(
        left, right, (((0,), (0,)), ((), ())), preferred_element_type=jnp.float32
    )


def unflatten(pieces):
    return (
        pieces[0].reshape(D, D),
        pieces[1].reshape(D, KVW),
        pieces[2].reshape(D, KVW),
        pieces[3].reshape(D, D),
        pieces[4].reshape(D, FF),
        pieces[5].reshape(D, FF),
        pieces[6].reshape(FF, D),
    )


def masked_scores(queries, key_rows, allowed):
    scores = jnp.einsum(
        "hgqd,hld->hgql", queries, key_rows, preferred_element_type=jnp.float32
    ) * HD ** (-0.5)
    return jnp.where(allowed, scores, MASKED)


def attend_forward(pieces):
    queries, key_rows, values, allowed = pieces
    scores = masked_scores(queries, key_rows, allowed)
    highest = jnp.max(scores, axis=-1, keepdims=True)
    weights = jnp.exp(scores - highest)
    summed = jnp.sum(weights, axis=-1, keepdims=True)
    shares = (weights / summed).astype(jnp.bfloat16)
    mixed_heads = jnp.einsum("hgql,hld->hgqd", shares, values, preferred_element_type=jnp.float32)
    return (mixed_heads, (highest + jnp.log(summed))[..., 0])


def attend_backward(pieces):
    queries, key_rows, values, allowed, log_total, grad_mixed = pieces
    scores = masked_scores(queries, key_rows, allowed)
    shares = jnp.exp(scores - log_total[..., None])
    shares_low = shares.astype(jnp.bfloat16)
    grad_shares = jnp.einsum(
        "hgqd,hld->hgql", grad_mixed, values, preferred_element_type=jnp.float32
    )
    inner = jnp.sum(shares * grad_shares, axis=-1, keepdims=True)
    grad_scores = (shares * (grad_shares - inner)).astype(jnp.bfloat16)
    score_scale = HD ** (-0.5)
    grad_queries = (
        jnp.einsum("hgql,hld->hgqd", grad_scores, key_rows, preferred_element_type=jnp.float32)
        * score_scale
    )
    grad_keys = (
        jnp.einsum("hgql,hgqd->hld", grad_scores, queries, preferred_element_type=jnp.float32)
        * score_scale
    )
    grad_values = jnp.einsum(
        "hgql,hgqd->hld", shares_low, grad_mixed, preferred_element_type=jnp.float32
    )
    return (grad_queries, grad_keys, grad_values)


def shards_flat(
    hidden_in,
    segments,
    w_query,
    w_key,
    w_value,
    w_out,
    w_gate,
    w_up,
    w_down,
    gain_vector,
    bias_vector,
    out_grad,
):
    seq_count = hidden_in.shape[0]
    block_len = hidden_in.shape[1]
    seq_len = block_len * lax.axis_size("seq")
    offset = lax.axis_index("seq") * block_len
    row_count = seq_count * block_len
    group_size = HEADS // KVH
    weights = unflatten(
        (
            lax.all_gather(w_query, ("dp", "seq"), axis=0, tiled=True),
            lax.all_gather(w_key, ("dp", "seq"), axis=0, tiled=True),
            lax.all_gather(w_value, ("dp", "seq"), axis=0, tiled=True),
            lax.all_gather(w_out, ("dp", "seq"), axis=0, tiled=True),
            lax.all_gather(w_gate, ("dp", "seq"), axis=0, tiled=True),
            lax.all_gather(w_up, ("dp", "seq"), axis=0, tiled=True),
            lax.all_gather(w_down, ("dp", "seq"), axis=0, tiled=True),
        )
    )
    query_mat, key_mat, value_mat, out_mat, gate_mat, up_mat, down_mat = weights
    gain_full, bias_full = (
        lax.all_gather(gain_vector, "seq", axis=0, tiled=True),
        lax.all_gather(bias_vector, "seq", axis=0, tiled=True),
    )
    first_gain = gain_full[:D].astype(jnp.float32)
    second_gain = gain_full[D:].astype(jnp.float32)
    bias_wide = bias_full.astype(jnp.float32)
    doc_all = lax.all_gather(segments, "seq", axis=1, tiled=True)
    places_all = doc_places(doc_all)
    cos_all, sin_all = rope_tables(places_all, HD)
    cos_here = lax.dynamic_slice_in_dim(cos_all, offset, block_len, 1)
    sin_here = lax.dynamic_slice_in_dim(sin_all, offset, block_len, 1)
    key_index = jnp.arange(seq_len)
    query_index = offset + jnp.arange(block_len)
    allowed = (segments[:, :, None] == doc_all[:, None, :]) & (
        key_index[None, None, :] <= query_index[None, :, None]
    )
    inputs = hidden_in.astype(jnp.float32).reshape(row_count, D)
    normed = rms_norm(inputs, first_gain).astype(jnp.bfloat16)
    query_pre = matmul(normed, query_mat) + bias_wide[:D]
    key_low = (
        (matmul(normed, key_mat) + bias_wide[D : D + KVW])
        .astype(jnp.bfloat16)
        .reshape(seq_count, block_len, KVW)
    )
    value_low = (
        (matmul(normed, value_mat) + bias_wide[D + KVW :])
        .astype(jnp.bfloat16)
        .reshape(seq_count, block_len, KVW)
    )
    key_all, value_all = (
        lax.all_gather(key_low, "seq", axis=1, tiled=True),
        lax.all_gather(value_low, "seq", axis=1, tiled=True),
    )
    key_heads = (
        key_all.astype(jnp.float32).reshape(seq_count, seq_len, KVH, HD).transpose(0, 2, 1, 3)
    )
    key_rot = turn(key_heads, cos_all[:, None], sin_all[:, None]).astype(jnp.bfloat16)
    value_heads = value_all.reshape(seq_count, seq_len, KVH, HD).transpose(0, 2, 1, 3)
    query_heads = query_pre.reshape(seq_count, block_len, KVH, group_size, HD).transpose(
        0, 2, 3, 1, 4
    )
    query_rot = turn(query_heads, cos_here[:, None, None], sin_here[:, None, None]).astype(
        jnp.bfloat16
    )
    mixed_heads, log_total = lax.map(attend_forward, (query_rot, key_rot, value_heads, allowed))
    mixed_rows = mixed_heads.transpose(0, 3, 1, 2, 4).reshape(row_count, D).astype(jnp.bfloat16)
    middle = inputs + matmul(mixed_rows, out_mat)
    normed_two = rms_norm(middle, second_gain).astype(jnp.bfloat16)
    gate_pre = matmul(normed_two, gate_mat)
    up_pre = matmul(normed_two, up_mat)
    activated = gated(gate_pre, up_pre).astype(jnp.bfloat16)
    result = middle + matmul(activated, down_mat)
    output = result.astype(jnp.bfloat16).reshape(seq_count, block_len, D)
    back_weights = unflatten(
        (
            lax.all_gather(w_query, ("dp", "seq"), axis=0, tiled=True),
            lax.all_gather(w_key, ("dp", "seq"), axis=0, tiled=True),
            lax.all_gather(w_value, ("dp", "seq"), axis=0, tiled=True),
            lax.all_gather(w_out, ("dp", "seq"), axis=0, tiled=True),
            lax.all_gather(w_gate, ("dp", "seq"), axis=0, tiled=True),
            lax.all_gather(w_up, ("dp", "seq"), axis=0, tiled=True),
            lax.all_gather(w_down, ("dp", "seq"), axis=0, tiled=True),
        )
    )
    query_mat, key_mat, value_mat, out_mat, gate_mat, up_mat, down_mat = back_weights
    grad_result = out_grad.astype(jnp.float32).reshape(row_count, D)
    grad_branch = grad_result.astype(jnp.bfloat16)
    grad_down_mat = contract_first(activated, grad_branch)
    grad_act = contract_last(grad_branch, down_mat)
    grad_gate_pre, grad_up_pre = jax.vjp(gated, gate_pre, up_pre)[1](grad_act)
    grad_gate_low = grad_gate_pre.astype(jnp.bfloat16)
    grad_up_low = grad_up_pre.astype(jnp.bfloat16)
    grad_gate_mat = contract_first(normed_two, grad_gate_low)
    grad_up_mat = contract_first(normed_two, grad_up_low)
    grad_normed_two = contract_last(grad_gate_low, gate_mat) + contract_last(grad_up_low, up_mat)
    grad_middle_part, grad_second_gain = jax.vjp(rms_norm, middle, second_gain)[1](grad_normed_two)
    grad_middle = grad_result + grad_middle_part
    grad_attn = grad_middle.astype(jnp.bfloat16)
    grad_out_mat = contract_first(mixed_rows, grad_attn)
    grad_mixed = contract_last(grad_attn, out_mat).astype(jnp.bfloat16)
    grad_mixed = grad_mixed.reshape(seq_count, block_len, KVH, group_size, HD).transpose(
        0, 2, 3, 1, 4
    )
    grad_query_rot, grad_key_rot, grad_value_heads = lax.map(
        attend_backward, (query_rot, key_rot, value_heads, allowed, log_total, grad_mixed)
    )
    grad_query_pre = unturn(grad_query_rot, cos_here[:, None, None], sin_here[:, None, None])
    grad_query_low = (
        grad_query_pre.transpose(0, 3, 1, 2, 4).reshape(row_count, D).astype(jnp.bfloat16)
    )
    grad_key_all = (
        unturn(grad_key_rot, cos_all[:, None], sin_all[:, None])
        .transpose(0, 2, 1, 3)
        .reshape(seq_count, seq_len, KVW)
    )
    grad_value_all = grad_value_heads.transpose(0, 2, 1, 3).reshape(seq_count, seq_len, KVW)
    grad_key_sum, grad_value_sum = (
        lax.psum_scatter(
            grad_key_all.astype(jnp.bfloat16), "seq", scatter_dimension=1, tiled=True
        ).astype(jnp.float32),
        lax.psum_scatter(
            grad_value_all.astype(jnp.bfloat16), "seq", scatter_dimension=1, tiled=True
        ).astype(jnp.float32),
    )
    grad_key_low = grad_key_sum.reshape(row_count, KVW).astype(jnp.bfloat16)
    grad_value_low = grad_value_sum.reshape(row_count, KVW).astype(jnp.bfloat16)
    grad_query_mat = contract_first(normed, grad_query_low)
    grad_key_mat = contract_first(normed, grad_key_low)
    grad_value_mat = contract_first(normed, grad_value_low)
    grad_normed = (
        contract_last(grad_query_low, query_mat)
        + contract_last(grad_key_low, key_mat)
        + contract_last(grad_value_low, value_mat)
    )
    grad_inputs_part, grad_first_gain = jax.vjp(rms_norm, inputs, first_gain)[1](grad_normed)
    input_grad = (grad_middle + grad_inputs_part).reshape(seq_count, block_len, D)
    count_dp = lax.axis_size("dp")
    count_seq = lax.axis_size("seq")
    owners = count_dp * count_seq
    owned = (
        lax.psum_scatter(
            grad_query_mat.reshape(owners, -1), ("dp", "seq"), scatter_dimension=0, tiled=True
        ),
        lax.psum_scatter(
            grad_key_mat.reshape(owners, -1), ("dp", "seq"), scatter_dimension=0, tiled=True
        ),
        lax.psum_scatter(
            grad_value_mat.reshape(owners, -1), ("dp", "seq"), scatter_dimension=0, tiled=True
        ),
        lax.psum_scatter(
            grad_out_mat.reshape(owners, -1), ("dp", "seq"), scatter_dimension=0, tiled=True
        ),
        lax.psum_scatter(
            grad_gate_mat.reshape(owners, -1), ("dp", "seq"), scatter_dimension=0, tiled=True
        ),
        lax.psum_scatter(
            grad_up_mat.reshape(owners, -1), ("dp", "seq"), scatter_dimension=0, tiled=True
        ),
        lax.psum_scatter(
            grad_down_mat.reshape(owners, -1), ("dp", "seq"), scatter_dimension=0, tiled=True
        ),
    )
    summed = tuple((piece.reshape(-1) for piece in owned))
    gain_total = jnp.concatenate([grad_first_gain, grad_second_gain])
    bias_total = jnp.concatenate(
        [
            jnp.sum(grad_query_low.astype(jnp.float32), axis=0),
            jnp.sum(grad_key_low.astype(jnp.float32), axis=0),
            jnp.sum(grad_value_low.astype(jnp.float32), axis=0),
        ]
    )
    gain_sum, bias_sum = lax.psum((gain_total, bias_total), ("dp", "seq"))
    seq_index = lax.axis_index("seq")
    gain_piece = gain_vector.shape[0]
    bias_piece = bias_vector.shape[0]
    gain_grad = lax.dynamic_slice_in_dim(gain_sum, seq_index * gain_piece, gain_piece)
    bias_grad = lax.dynamic_slice_in_dim(bias_sum, seq_index * bias_piece, bias_piece)
    return (
        output,
        input_grad,
        summed[0],
        summed[1],
        summed[2],
        summed[3],
        summed[4],
        summed[5],
        summed[6],
        gain_grad,
        bias_grad,
    )


def spread(rows, block, spare):
    place = jnp.arange(rows)
    place = place // block * spare + place % block
    width = rows // block * spare
    return (place[:, None] == jnp.arange(width)[None, :]).astype(jnp.bfloat16)


def round_up(value, step):
    return -(-value // step) * step


def shards_split(
    hidden_in,
    segments,
    w_query,
    w_key,
    w_value,
    w_out,
    w_gate,
    w_up,
    w_down,
    gain_vector,
    bias_vector,
    out_grad,
):
    low = jnp.bfloat16
    seq_count, block_len, _ = hidden_in.shape
    count_dp = lax.axis_size("dp")
    count_seq = lax.axis_size("seq")
    owners = count_dp * count_seq
    dp_index = lax.axis_index("dp")
    seq_index = lax.axis_index("seq")
    seq_len = block_len * count_seq
    offset = seq_index * block_len
    row_count = seq_count * block_len
    group_size = HEADS // KVH
    own_rows = D // owners
    block = round_up(own_rows + 1, 16)
    own_units = FF // owners
    unit_block = round_up(own_units, 16)
    units = count_dp * unit_block
    gain_piece = gain_vector.shape[0]
    bias_piece = bias_vector.shape[0]
    both = ("dp", "seq")

    attn_width = 2 * D + 2 * KVW
    attn_rows = jnp.concatenate(
        [
            w_query.reshape(own_rows, D),
            w_key.reshape(own_rows, KVW),
            w_value.reshape(own_rows, KVW),
            w_out.reshape(own_rows, D),
        ],
        axis=1,
    )
    small = jnp.concatenate([gain_vector, bias_vector, segments.astype(low).reshape(-1)])
    small = jnp.pad(small, (0, attn_width - small.shape[0]))[None]
    attn_rows = jnp.concatenate(
        [attn_rows, small, jnp.zeros((block - own_rows - 1, attn_width), low)], axis=0
    )
    attn_all = lax.all_gather(attn_rows, both, axis=0, tiled=True)
    pick = spread(D, own_rows, block)

    def to_all_dp(piece):
        copies = jnp.broadcast_to(piece[None], (count_dp, *piece.shape))
        return lax.all_to_all(copies, "dp", 0, 0, tiled=True).reshape(-1, piece.shape[1])

    def by_user(flat):
        parts = flat.reshape(own_rows, count_dp, count_seq, own_units).transpose(2, 0, 1, 3)
        parts = jnp.pad(
            parts, ((0, 0), (0, block - own_rows), (0, 0), (0, unit_block - own_units))
        )
        return parts.reshape(count_seq, block, units)

    gate_up_own = jnp.concatenate([by_user(w_gate), by_user(w_up)], axis=2)
    gate_up_own = lax.all_to_all(gate_up_own, "seq", 0, 0, tiled=True)
    gate_up_all = to_all_dp(gate_up_own.reshape(count_seq * block, 2 * units))
    down_own = jnp.pad(w_down.reshape(own_units, D), ((0, unit_block - own_units), (0, 0)))
    down_mat = to_all_dp(down_own)
    attn_all, gate_up_all, down_mat = lax.optimization_barrier((attn_all, gate_up_all, down_mat))
    small_all = attn_all.reshape(owners, block, attn_width)[:, own_rows]
    gain_full = small_all[:count_seq, :gain_piece].reshape(-1).astype(jnp.float32)
    bias_wide = (
        small_all[:count_seq, gain_piece : gain_piece + bias_piece].reshape(-1).astype(jnp.float32)
    )
    small_here = lax.dynamic_slice_in_dim(small_all, dp_index * count_seq, count_seq, 0)
    doc_all = (
        small_here[:, gain_piece + bias_piece : gain_piece + bias_piece + row_count]
        .astype(jnp.int32)
        .reshape(count_seq, seq_count, block_len)
        .transpose(1, 0, 2)
        .reshape(seq_count, seq_len)
    )
    first_gain = gain_full[:D]
    second_gain = gain_full[D:]
    attn_mat = matmul(pick, attn_all).astype(low)
    qkv_mat = attn_mat[:, : D + 2 * KVW]
    out_mat = attn_mat[:, D + 2 * KVW :]
    gate_up_mat = matmul(pick, gate_up_all).astype(low)

    places_all = doc_places(doc_all)
    cos_all, sin_all = rope_tables(places_all, HD)
    cos_here = lax.dynamic_slice_in_dim(cos_all, offset, block_len, 1)
    sin_here = lax.dynamic_slice_in_dim(sin_all, offset, block_len, 1)
    key_index = jnp.arange(seq_len)
    query_index = offset + jnp.arange(block_len)
    allowed = (segments[:, :, None] == doc_all[:, None, :]) & (
        key_index[None, None, :] <= query_index[None, :, None]
    )
    inputs = hidden_in.astype(jnp.float32).reshape(row_count, D)
    normed = rms_norm(inputs, first_gain).astype(low)
    qkv_pre = matmul(normed, qkv_mat) + bias_wide
    query_pre = qkv_pre[:, :D]
    key_value_low = qkv_pre[:, D:].astype(low).reshape(seq_count, block_len, 2 * KVW)
    key_value_all = lax.all_gather(key_value_low, "seq", axis=1, tiled=True)
    key_value_all, grad_branch_own = lax.optimization_barrier((key_value_all, out_grad))
    grad_branch_all = lax.all_gather(
        grad_branch_own.reshape(row_count, D), "seq", axis=0, tiled=True
    )
    key_all = key_value_all[..., :KVW]
    value_all = key_value_all[..., KVW:]
    key_heads = (
        key_all.astype(jnp.float32).reshape(seq_count, seq_len, KVH, HD).transpose(0, 2, 1, 3)
    )
    key_rot = turn(key_heads, cos_all[:, None], sin_all[:, None]).astype(low)
    value_heads = value_all.reshape(seq_count, seq_len, KVH, HD).transpose(0, 2, 1, 3)
    query_heads = query_pre.reshape(seq_count, block_len, KVH, group_size, HD).transpose(
        0, 2, 3, 1, 4
    )
    query_rot = turn(query_heads, cos_here[:, None, None], sin_here[:, None, None]).astype(low)
    mixed_parts = []
    log_totals = []
    for one in range(seq_count):
        mixed_heads, log_total = attend_forward(
            (query_rot[one], key_rot[one], value_heads[one], allowed[one])
        )
        mixed_parts.append(mixed_heads.transpose(2, 0, 1, 3).reshape(block_len, D).astype(low))
        log_totals.append(log_total)
    mixed_rows = jnp.concatenate(mixed_parts, axis=0)
    middle = inputs + matmul(mixed_rows, out_mat)
    normed_two = rms_norm(middle, second_gain).astype(low)

    normed_all = lax.all_gather(normed_two, "seq", axis=0, tiled=True)
    gate_up_pre = matmul(normed_all, gate_up_mat)
    gate_pre = gate_up_pre[:, :units]
    up_pre = gate_up_pre[:, units:]
    activated = gated(gate_pre, up_pre).astype(low)
    grad_act = contract_last(grad_branch_all, down_mat)
    grad_gate_pre, grad_up_pre = jax.vjp(gated, gate_pre, up_pre)[1](grad_act)
    grad_gate_up = jnp.concatenate([grad_gate_pre.astype(low), grad_up_pre.astype(low)], axis=1)
    grad_normed_part = contract_last(grad_gate_up, gate_up_mat).astype(low)
    grad_normed_two = lax.psum_scatter(
        grad_normed_part, "seq", scatter_dimension=0, tiled=True
    ).astype(jnp.float32)
    branch_part = matmul(activated, down_mat).astype(low)
    branch = lax.psum_scatter(branch_part, "seq", scatter_dimension=0, tiled=True)
    output = (middle + branch.astype(jnp.float32)).astype(low).reshape(seq_count, block_len, D)

    grad_gate_up_mat = contract_first(normed_all, grad_gate_up).astype(low)
    grad_gate_up_mat = contract_first(pick, grad_gate_up_mat).astype(low)
    grad_down_mat = contract_first(activated, grad_branch_all).astype(low)
    grad_gate_up_sum = lax.psum_scatter(grad_gate_up_mat, "dp", scatter_dimension=0, tiled=True)
    grad_result = out_grad.astype(jnp.float32).reshape(row_count, D)
    grad_middle_part, grad_second_gain = jax.vjp(rms_norm, middle, second_gain)[1](grad_normed_two)
    grad_middle = grad_result + grad_middle_part
    grad_attn = grad_middle.astype(low)
    pick_rows = lambda values: matmul(values, pick).astype(low)
    grad_out_mat = contract_first(pick_rows(mixed_rows), grad_attn).astype(low)
    grad_down_out = jnp.concatenate(
        [
            grad_down_mat.reshape(count_dp, unit_block, D),
            grad_out_mat.reshape(count_dp, count_seq * block, D),
        ],
        axis=1,
    ).reshape(-1, D)
    grad_down_out = lax.psum_scatter(grad_down_out, "dp", scatter_dimension=0, tiled=True)
    grad_down = grad_down_out[:own_units].astype(jnp.float32).reshape(-1)
    grad_owned = jnp.concatenate([grad_gate_up_sum, grad_down_out[unit_block:]], axis=1)
    grad_owned = lax.all_to_all(
        grad_owned.reshape(count_seq, block, 2 * units + D), "seq", 0, 0, tiled=True
    )
    grad_gate_up_own = (
        grad_owned[:, :own_rows, : 2 * units]
        .reshape(count_seq, own_rows, 2, count_dp, unit_block)[..., :own_units]
        .transpose(2, 1, 3, 0, 4)
        .reshape(2, -1)
        .astype(jnp.float32)
    )
    grad_out_sum = jnp.sum(grad_owned[:, :own_rows, 2 * units :].astype(jnp.float32), axis=0)
    grad_mixed = contract_last(grad_attn, out_mat).astype(low)
    grad_mixed = grad_mixed.reshape(seq_count, block_len, KVH, group_size, HD).transpose(
        0, 2, 3, 1, 4
    )
    grad_query_parts = []
    grad_key_value_parts = []
    for one in range(seq_count):
        grad_query_rot, grad_key_rot, grad_value_heads = attend_backward(
            (
                query_rot[one],
                key_rot[one],
                value_heads[one],
                allowed[one],
                log_totals[one],
                grad_mixed[one],
            )
        )
        grad_query_pre = unturn(grad_query_rot, cos_here[one], sin_here[one])
        grad_query_parts.append(
            grad_query_pre.transpose(2, 0, 1, 3).reshape(block_len, D).astype(low)
        )
        grad_key_pre = unturn(grad_key_rot, cos_all[one], sin_all[one])
        grad_key_value_parts.append(
            jnp.concatenate([grad_key_pre, grad_value_heads], axis=0)
            .transpose(1, 0, 2)
            .reshape(seq_len, 2 * KVW)
            .astype(low)
        )
    grad_query_low = jnp.concatenate(grad_query_parts, axis=0)
    grad_key_value = jnp.stack(grad_key_value_parts)
    grad_key_value_low = lax.psum_scatter(
        grad_key_value, "seq", scatter_dimension=1, tiled=True
    ).reshape(row_count, 2 * KVW)
    grad_qkv_low = jnp.concatenate([grad_query_low, grad_key_value_low], axis=1)
    grad_qkv_mat = contract_first(pick_rows(normed), grad_qkv_low)
    grad_normed = contract_last(grad_qkv_low, qkv_mat)
    grad_inputs_part, grad_first_gain = jax.vjp(rms_norm, inputs, first_gain)[1](grad_normed)
    input_grad = (grad_middle + grad_inputs_part).reshape(seq_count, block_len, D)
    gain_total = jnp.concatenate([grad_first_gain, grad_second_gain]).reshape(count_seq, gain_piece)
    bias_total = jnp.sum(grad_qkv_low.astype(jnp.float32), axis=0).reshape(count_seq, bias_piece)
    small_total = jnp.concatenate([gain_total, bias_total], axis=1)
    small_total = jnp.tile(small_total, (count_dp, 1))[:, None]
    qkv_width = D + 2 * KVW
    small_total = jnp.pad(
        small_total,
        (
            (0, 0),
            (own_rows, block - own_rows - 1),
            (0, qkv_width - gain_piece - bias_piece),
        ),
    )
    grad_qkv_mat = grad_qkv_mat + small_total.reshape(owners * block, qkv_width)
    grad_qkv_part = lax.psum_scatter(
        grad_qkv_mat.astype(low), "dp", scatter_dimension=0, tiled=True
    )
    grad_qkv_part = lax.all_to_all(
        grad_qkv_part.reshape(count_seq, block, qkv_width), "seq", 0, 0, tiled=True
    )
    grad_qkv_sum = jnp.sum(grad_qkv_part.astype(jnp.float32), axis=0)
    gain_grad = grad_qkv_sum[own_rows, :gain_piece]
    bias_grad = grad_qkv_sum[own_rows, gain_piece : gain_piece + bias_piece]
    grad_qkv_sum = grad_qkv_sum[:own_rows]
    return (
        output,
        input_grad,
        grad_qkv_sum[:, :D].reshape(-1),
        grad_qkv_sum[:, D : D + KVW].reshape(-1),
        grad_qkv_sum[:, D + KVW :].reshape(-1),
        grad_out_sum.reshape(-1),
        grad_gate_up_own[0],
        grad_gate_up_own[1],
        grad_down,
        gain_grad,
        bias_grad,
    )


def solution(mesh):
    in_specs = (
        P("dp", "seq", None),
        P("dp", "seq"),
        P(("dp", "seq")),
        P(("dp", "seq")),
        P(("dp", "seq")),
        P(("dp", "seq")),
        P(("dp", "seq")),
        P(("dp", "seq")),
        P(("dp", "seq")),
        P("seq"),
        P("seq"),
        P("dp", "seq", None),
    )
    out_specs = (
        P("dp", "seq", None),
        P("dp", "seq", None),
        P(("dp", "seq")),
        P(("dp", "seq")),
        P(("dp", "seq")),
        P(("dp", "seq")),
        P(("dp", "seq")),
        P(("dp", "seq")),
        P(("dp", "seq")),
        P("seq"),
        P("seq"),
    )
    owners = mesh.size
    whole_rows = D % owners == 0 and FF % owners == 0
    shards = shards_split if whole_rows else shards_flat
    return jax.shard_map(shards, mesh=mesh, in_specs=in_specs, out_specs=out_specs, check_vma=False)
```
